32 devices in a mesh: dp: 8 (over z, y), mp: 4 (over x, core).
Axes of the slice: x: 2, y: 2, z: 4, core: 2. Of those that a mesh axis runs over, the one named last changes fastest.
Arguments:
- features: bfloat16 [2, 2048, 1536], P(None, 'dp'), may hold values from -30 to 30
- proj_weight: bfloat16 [1536, 4096], P(None, 'mp'), may hold values from -0.15625 to 0.15625
Outputs:
- loss_value: float32 [], replicated
- feature_grad: bfloat16 [2, 2048, 1536], P(None, 'dp', 'mp')
The draws below stay inside these ranges and needn't reach their ends.
All inputs are finite; a program needn't handle non-finite values.
Results may differ from the reference program's by a relative error of at most 0.012.
Values may be sent and summed in bfloat16 or wider, within the bound.
A program may use at most 128 MiB of HBM per device.

```python
import jax
import jax.numpy as jnp
from jax import lax

D_IN = 1536
EMB = 4096
BATCH = 2048
N_MP = 4


def draw_features(key, part):
    key = jax.random.fold_in(key, 17)
    k_base, k_noise, k_rough, k_offset = jax.random.split(key, 4)
    shape = (BATCH, D_IN)
    position = jnp.arange(BATCH, dtype=jnp.float32) / max(BATCH - 1, 1)
    base = jax.random.truncated_normal(k_base, -4.0, 4.0, shape, jnp.float32)
    noise = jax.random.truncated_normal(k_noise, -4.0, 4.0, shape, jnp.float32)
    rising = 1.0 + 2.0 * position
    offset = 1.5 * jax.random.truncated_normal(k_offset, -2.0, 2.0, (1, D_IN), jnp.float32)
    rough = jax.random.uniform(k_rough, (BATCH, 1), jnp.float32, 0.7, 1.4)
    row_scale = rising[:, None] * rough
    first = base * row_scale + offset
    second = (0.8 * base + 0.6 * noise) * row_scale + offset
    return jnp.stack([first, second]).astype(jnp.bfloat16)


def block_levels(key, extent, cuts, least, top_value):
    factor_of, own = 1.0, jax.random.fold_in(key, 6)
    for axis_at, shards_of in cuts:
        heights = jnp.exp(jax.random.uniform(jax.random.fold_in(own, axis_at), (shards_of,), jnp.float32, least / len(cuts), top_value / len(cuts)))
        factor_of = factor_of * jnp.repeat(heights, extent[axis_at] // shards_of).reshape([-1 if axis == axis_at else 1 for axis in range(len(extent))])
    return factor_of


def bell_draw(own_key, dims, scale, bound, pieces=(), kind=jnp.bfloat16):
    drawn = jax.random.normal(own_key, dims, jnp.float32) * scale
    if len(pieces) > 0:
        drawn = block_levels(own_key, dims, pieces, -0.22, 0.18) * drawn
    return jnp.clip(drawn, min=-bound, max=bound).astype(kind)


def setup_inputs(seed: int = 0) -> dict:
    key_list = jax.random.split(jax.random.key(seed), 3)
    return {
        "features": draw_features(jax.random.fold_in(key_list[2], 71), 0),
        "proj_weight": bell_draw(key_list[1], (D_IN, EMB), D_IN ** -0.5, 0.15625, ((1, 4),)),
    }


def reference(features, proj_weight):
    flat = features.reshape(2 * BATCH, D_IN)
    pre = jnp.dot(flat, proj_weight, preferred_element_type=jnp.float32).reshape(2, BATCH, EMB)
    mean = lax.optimization_barrier(jnp.sum(pre, axis=1, keepdims=True)) / BATCH
    centred = pre - mean
    spread = lax.optimization_barrier(jnp.sum(centred * centred, axis=1, keepdims=True)) / BATCH
    scale_inv = lax.rsqrt(spread + 1e-05)
    normed = centred * scale_inv
    embed = normed.astype(jnp.bfloat16)
    corr = jnp.dot(embed[0].T, embed[1], preferred_element_type=jnp.float32) / BATCH
    on_diag = jnp.eye(EMB, dtype=jnp.bool_)
    miss = 1.0 - corr
    loss_value = jnp.sum(jnp.where(on_diag, miss * miss, 0.0051 * corr * corr)) / EMB
    grad_corr = jnp.where(on_diag, -2.0 * miss, 2.0 * 0.0051 * corr).astype(jnp.bfloat16)
    grad_a = jnp.dot(embed[1], grad_corr.T, preferred_element_type=jnp.float32)
    block = EMB // N_MP
    grad_b = jnp.zeros((BATCH, EMB), jnp.float32)
    for member in range(N_MP):
        piece = jnp.dot(embed[0][:, member * block:(member + 1) * block], grad_corr[member * block:(member + 1) * block, :], preferred_element_type=jnp.float32)
        grad_b = grad_b + piece.astype(jnp.bfloat16).astype(jnp.float32)
    grads = jnp.stack([grad_a, grad_b])
    first_sum = lax.optimization_barrier(jnp.sum(grads, axis=1, keepdims=True))
    second_sum = lax.optimization_barrier(jnp.sum(grads * normed, axis=1, keepdims=True))
    pre_grad = (scale_inv * (grads - first_sum / BATCH - normed * second_sum / BATCH)).astype(jnp.bfloat16)
    flat_grad = pre_grad.reshape(2 * BATCH, EMB)
    back = jnp.zeros((2 * BATCH, D_IN), jnp.float32)
    for member in range(N_MP):
        piece = jnp.dot(flat_grad[:, member * block:(member + 1) * block], proj_weight[:, member * block:(member + 1) * block].T, preferred_element_type=jnp.float32)
        back = back + piece.astype(jnp.bfloat16).astype(jnp.float32)
    feature_grad = back.reshape(2, BATCH, D_IN).astype(jnp.bfloat16)
    return (loss_value, feature_grad)
```

```python
import functools

import jax
import jax.numpy as jnp
from jax import lax
from jax.sharding import PartitionSpec as P

BF = jnp.bfloat16
F32 = jnp.float32


def lanes(parts):
    flat = jnp.concatenate([p.reshape(-1) for p in parts])
    return jnp.pad(flat, (0, -flat.shape[0] % 1024)).reshape(-1, 128)


def on_device(n, n_mp, features, proj_weight):
    rows, d_in = features.shape[1:]
    width = proj_weight.shape[1]
    part = d_in // n_mp
    batch = float(rows * n)
    few = float(rows)
    m = lax.axis_index("mp")

    flat = features.reshape(2 * rows, d_in)
    pre = jnp.dot(flat, proj_weight, preferred_element_type=F32).reshape(2, rows, width)
    f_mean = jnp.mean(features.astype(F32), axis=1)
    p_mean = jnp.mean(pre, axis=1)
    near = pre - p_mean[:, None, :]
    squares = jnp.sum(near * near, axis=1)
    cross = jnp.sum(near[0] * near[1], axis=0)
    stats = lax.all_gather(lanes([f_mean, p_mean, squares, cross]), "dp")
    stats = stats.reshape(n, -1)
    cuts = [2 * d_in, 2 * d_in + 2 * width, 2 * d_in + 4 * width]
    f_means = stats[:, : cuts[0]].reshape(n, 2, d_in)
    p_means = stats[:, cuts[0] : cuts[1]].reshape(n, 2, width)
    all_squares = stats[:, cuts[1] : cuts[2]].reshape(n, 2, width)
    all_cross = stats[:, cuts[2] : cuts[2] + width]
    f_all = jnp.mean(f_means, axis=0)
    mean = jnp.mean(p_means, axis=0)
    off = p_means - mean
    spread = (jnp.sum(all_squares, axis=0) + few * jnp.sum(off * off, axis=0)) / batch
    scale = lax.rsqrt(spread + 1e-05)
    corr_diag = (
        (jnp.sum(all_cross, axis=0) + few * jnp.sum(off[:, 0] * off[:, 1], axis=0)) / batch * scale[0] * scale[1]
    )
    extra = (2.0 - 2.0 * 0.0051) * corr_diag - 2.0

    f_a = lax.dynamic_slice_in_dim(features[0], m * part, part, 1)
    ma_here = lax.dynamic_slice_in_dim(f_mean[0], m * part, part, 0)
    ma_all = lax.dynamic_slice_in_dim(f_all[0], m * part, part, 0)
    outer = few * (
        ma_here[:, None] * f_mean[1][None, :]
        - (ma_here - ma_all)[:, None] * (f_mean[1] - f_all[1])[None, :]
    )
    sig = lax.dot_general(f_a, features[1], (((0,), (0,)), ((), ())), preferred_element_type=F32) - outer
    sig = lax.psum_scatter(sig / batch, "dp", scatter_dimension=0, tiled=True).astype(BF)

    centred = pre - mean[:, None, :]
    normed = centred * scale[:, None, :]
    embed = normed.astype(BF)
    scaled = (normed * scale[:, None, :]).astype(BF).reshape(2 * rows, width)
    u = lax.dot_general(scaled, proj_weight, (((1,), (1,)), ((), ())), preferred_element_type=F32)
    u = lax.psum(u.astype(BF), "mp")
    sig = lax.all_gather(sig, ("mp", "dp"), axis=0, tiled=True)

    v_a = lax.dot_general(u[rows:], sig, (((1,), (1,)), ((), ())), preferred_element_type=F32).astype(BF)
    v_b = jnp.dot(u[:rows], sig, preferred_element_type=F32).astype(BF)
    h = jnp.dot(jnp.concatenate([v_a, v_b]), proj_weight, preferred_element_type=F32)
    h = h.reshape(2, rows, width) * scale[:, None, :]
    grads = 2.0 * 0.0051 * h + extra * embed[::-1].astype(F32)
    first = jnp.sum(grads, axis=1)
    second = jnp.sum(grads * normed, axis=1)
    row_squares = jnp.sum(h[0] * normed[0], axis=0)
    sums = lax.psum(lanes([first, second, row_squares]), "dp").reshape(-1) / batch
    first = sums[: 2 * width].reshape(2, width)
    second = sums[2 * width : 4 * width].reshape(2, width)
    row_squares = sums[4 * width : 5 * width]
    loss_part = jnp.sum((1.0 - corr_diag) ** 2 + 0.0051 * (row_squares - corr_diag**2))
    pre_grad = (scale[:, None, :] * (grads - first[:, None, :] - normed * second[:, None, :])).astype(BF)
    pre_grad = pre_grad.reshape(2 * rows, width)
    back = lax.dot_general(pre_grad, proj_weight, (((1,), (1,)), ((), ())), preferred_element_type=F32)
    back = lax.psum_scatter(back.astype(BF), "mp", scatter_dimension=1, tiled=True)
    loss_value = lax.psum(loss_part, "mp") / float(width * n_mp)
    feature_grad = back.reshape(2, rows, part)
    return loss_value, feature_grad


def solution(mesh):
    placed = (P(None, "dp", None), P(None, "mp"))
    return jax.shard_map(
        functools.partial(on_device, mesh.shape["dp"], mesh.shape["mp"]),
        mesh=mesh,
        in_specs=placed,
        out_specs=(P(), P(None, "dp", "mp")),
        check_vma=False,
    )
```
